32 devices in a mesh: beam: 4 (over y, x), chan: 8 (over z, core).
Axes of the slice: x: 2, y: 2, z: 4, core: 2. Of those that a mesh axis runs over, the one named last changes fastest.
Arguments:
- intensities: bfloat16 [32, 8192, 128], P(None, ('beam', 'chan')), may hold values from -6 to 6
- lower_index: int32 [10, 1024], replicated, may hold values from 0 to 511, as said below
- upper_index: int32 [10, 1024], replicated, may hold values from 0 to 511, as said below
- delay_shift: int32 [10, 1024], replicated, may hold values from 0 to 512, as said below
- widths: int32 [8], replicated, may hold values from 1 to 64, as said below
- max_delay: int32 [32], P(('beam', 'chan')), may hold values from 256 to 1023
Outputs:
- snr: float32 [32, 8, 1024], P(('beam', 'chan'))
The draws below stay inside these ranges and needn't reach their ends.
Inputs may be any that keep to these rules, and one draw needn't show every extreme that they name: `lower_index`: at level l and row r, with d = r mod 2^(l+1), the entry is either floor(d / 2) or min(floor((d + 1) / 2), 2^l - 1). `upper_index`: at level l and row r, with d = r mod 2^(l+1), the entry is either floor(d / 2) or min(floor((d + 1) / 2), 2^l - 1). `delay_shift`: at level l the shift is at most 2^l. Distinct widths; 1 and 64 are always among them.
All inputs are finite; a program needn't handle non-finite values.
Results may differ from the reference program's by a relative error of at most 0.0003.
Values sent between devices are 32-bit elements; how exact they have to be, the bound alone decides.
A program may use at most 64 MiB of HBM per device.

```python
import jax
import jax.numpy as jnp
from jax import lax

C = 8192
DM_LOG = 10
DM_TOP = 1024
SUB0 = 8
SAMPLES = 128
BEAMS = 32
NBOX = 8
MAXW = 64


def fdmt_tables(key):
    level_ids = jnp.arange(DM_LOG, dtype=jnp.int32)[:, None]
    row_ids = jnp.arange(DM_TOP, dtype=jnp.int32)[None, :]
    rows_now = jnp.left_shift(jnp.int32(1), level_ids + 1)
    rows_before = rows_now // 2
    trial = row_ids % rows_now
    coin = jax.random.randint(jax.random.fold_in(key, 11), (DM_LOG, DM_TOP), 0, 2, dtype=jnp.int32)
    lower_part = jnp.minimum((trial + coin) // 2, rows_before - 1)
    upper_part = jnp.minimum(trial - lower_part, rows_before - 1)
    moved = lower_part + trial % 2
    return (lower_part.astype(jnp.int32), upper_part.astype(jnp.int32), moved.astype(jnp.int32))


def draw_lower_index(key, part):
    return fdmt_tables(key)[0]


def draw_upper_index(key, part):
    return fdmt_tables(key)[1]


def draw_delay_shift(key, part):
    return fdmt_tables(key)[2]


def draw_widths(key, part):
    inner = jax.random.permutation(jax.random.fold_in(key, 5), MAXW - 2)[:NBOX - 2] + 2
    values = jnp.concatenate([jnp.array([1, MAXW], dtype=jnp.int32), inner.astype(jnp.int32)])
    order = jax.random.permutation(jax.random.fold_in(key, 6), NBOX)
    return values[order].astype(jnp.int32)


def draw_max_delay(key, part):
    values = jax.random.randint(jax.random.fold_in(key, 21), (BEAMS,), DM_TOP // 4, DM_TOP, dtype=jnp.int32)
    first_pick = jax.random.randint(jax.random.fold_in(key, 22), (), 0, BEAMS, dtype=jnp.int32)
    second_pick = (first_pick + 1 + jax.random.randint(jax.random.fold_in(key, 23), (), 0, BEAMS - 1, dtype=jnp.int32)) % BEAMS
    places = jnp.arange(BEAMS, dtype=jnp.int32)
    values = jnp.where(places == first_pick, DM_TOP - 1, values)
    values = jnp.where(places == second_pick, DM_TOP // 4, values)
    return values.astype(jnp.int32)


def levels(rng, extent, split, least, largest):
    gain = 1.0
    for dim, shards_of in split:
        heights = jax.random.uniform(jax.random.fold_in(jax.random.fold_in(rng, 6), dim), (shards_of,), jnp.float32, least / len(split), largest / len(split))
        gain = gain * jnp.repeat(jnp.exp(heights), extent[dim] // shards_of).reshape((-1,) + (1,) * (len(extent) - 1 - dim))
    return gain


def noise(key, shape, deviation, most, shards=(), kind=jnp.bfloat16):
    values = jax.random.normal(key, shape, jnp.float32) * deviation
    if len(shards) > 0:
        values = levels(key, shape, shards, -0.22, 0.18) * values
    return jnp.clip(values, min=-most, max=most).astype(kind)


def setup_inputs(seed: int = 0) -> dict:
    keys = jax.random.split(jax.random.key(seed), 7)
    intensities = noise(keys[0], (BEAMS, C, SAMPLES), 1.0, 6.0, ((1, 32),))
    lower_index = draw_lower_index(jax.random.fold_in(keys[6], 71), 0)
    upper_index = draw_upper_index(jax.random.fold_in(keys[6], 71), 0)
    delay_shift = draw_delay_shift(jax.random.fold_in(keys[6], 71), 0)
    widths = draw_widths(jax.random.fold_in(keys[6], 71), 0)
    max_delay = draw_max_delay(jax.random.fold_in(keys[6], 71), 0)
    return {"intensities": intensities, "lower_index": lower_index, "upper_index": upper_index, "delay_shift": delay_shift, "widths": widths, "max_delay": max_delay}


def delayed(values, amounts):
    samples_here = values.shape[-1]
    time_index = jnp.arange(samples_here, dtype=jnp.int32)
    source = time_index[None, None, :] - amounts[..., None]
    fetched = jnp.take_along_axis(values, jnp.maximum(source, 0).astype(jnp.int32), axis=-1)
    return jnp.where(source >= 0, fetched, jnp.zeros_like(fetched))

def pick_rows(state_part, index_table):
    return jax.vmap(lambda block_in, index_in: jnp.take(block_in, index_in, axis=0))(state_part, index_table)

def fdmt_beam(block, lower_index, upper_index, delay_shift):
    state = lax.optimization_barrier(jnp.sum(block.reshape(DM_TOP, SUB0, SAMPLES), axis=1, dtype=jnp.float32))[:, None, :]
    for merge_step in range(DM_LOG):
        pair_count = state.shape[0] // 2
        new_rows = 2 * state.shape[1]
        lower_table = lower_index[merge_step].reshape(pair_count, new_rows)
        upper_table = upper_index[merge_step].reshape(pair_count, new_rows)
        shift_table = delay_shift[merge_step].reshape(pair_count, new_rows)
        lower_rows = pick_rows(state[0::2], lower_table)
        upper_rows = pick_rows(state[1::2], upper_table)
        state = lower_rows + delayed(upper_rows, shift_table)
    return state[0]

def scores(trials, widths, limit):
    running = jnp.cumsum(trials, axis=-1)
    padded = jnp.concatenate([jnp.zeros((DM_TOP, MAXW), running.dtype), running], axis=-1)

    def one_width(width):
        earlier = lax.dynamic_slice_in_dim(padded, (MAXW - width).astype(jnp.int32), SAMPLES, axis=1)
        boxcar = running - earlier
        center = lax.optimization_barrier(jnp.mean(boxcar, axis=-1, keepdims=True))
        offset = boxcar - center
        spread = lax.optimization_barrier(jnp.mean(offset * offset, axis=-1, keepdims=True))
        return lax.optimization_barrier(jnp.max(offset / jnp.sqrt(spread + 1e-05), axis=-1))
    table = lax.map(one_width, widths)
    keep_rows = jnp.arange(DM_TOP, dtype=jnp.int32) <= limit
    return jnp.where(keep_rows[None, :], table, jnp.zeros_like(table))

def reference(intensities, lower_index, upper_index, delay_shift, widths, max_delay):

    def one_beam(packed):
        block, limit = packed
        trials = fdmt_beam(block, lower_index, upper_index, delay_shift)
        return scores(trials, widths, limit)
    return lax.map(one_beam, (intensities, max_delay))
```

```python
import functools

import jax
import jax.numpy as jnp
from jax import lax
from jax.experimental import pallas as pl
from jax.experimental.pallas import tpu as pltpu
from jax.sharding import PartitionSpec as P

SUB0 = 8
ROWS = 8
MESH = pl.DeviceIdType.MESH


def xor(left, right, size):
    total = 0
    for bit in range(size.bit_length() - 1):
        step = 1 << bit
        total = total + step * ((left // step + right // step) % 2)
    return total


def take(values, index, axis):
    return jnp.take_along_axis(values, index, axis=axis, mode="promise_in_bounds")


def build_indices(levels, bands, samples, lower_ref, upper_ref, shift_ref, low_at, up_at, time_at):
    depth = 16
    zeros = jnp.zeros((depth - levels, bands), jnp.int32)
    lower = jnp.concatenate([lower_ref[...], zeros], axis=0)
    upper = jnp.concatenate([upper_ref[...], zeros], axis=0)
    shift = jnp.concatenate([shift_ref[...], zeros], axis=0)
    level = lax.broadcasted_iota(jnp.int32, (depth, bands), 0)
    row = lax.broadcasted_iota(jnp.int32, (depth, bands), 1)
    width = jnp.left_shift(jnp.int32(2), level)
    trial = row & (width - 1)
    inside = (row & (ROWS - 1)) - trial
    skip = jnp.where(level >= 4, 4 * (trial // ROWS), 0)
    lower = jnp.where(level <= 2, inside + lower, lower - skip) & (ROWS - 1)
    upper = jnp.where(level <= 2, inside + width // 2 + upper, upper - skip) & (ROWS - 1)
    packed = jnp.concatenate(
        [(lower + ROWS * upper).astype(jnp.float32), jnp.minimum(shift, samples).astype(jnp.float32)],
        axis=0,
    ).astype(jnp.bfloat16)
    entry = lax.broadcasted_iota(jnp.int32, (2 * depth, samples), 0)
    time = lax.broadcasted_iota(jnp.int32, (bands, samples), 1)
    for step in range(levels):
        spread = jnp.where(entry == step, 256.0, jnp.where(entry == depth + step, 1.0, 0.0))
        value = lax.dot_general(
            packed,
            spread.astype(jnp.bfloat16),
            (((0,), (0,)), ((), ())),
            preferred_element_type=jnp.float32,
        ).astype(jnp.int32)
        low_at[step] = (value >> 8) & (ROWS - 1)
        up_at[step] = value >> 11
        time_at[step] = time - (value & 255)


def merge(lower, upper, step, rows, low_at, up_at, time_at):
    samples = lower.shape[-1]
    when = time_at[step, rows]
    upper = take(upper, up_at[step, rows], 0)
    upper = take(upper, when & (samples - 1), 1)
    return take(lower, low_at[step, rows], 0) + jnp.where(when >= 0, upper, 0.0)


def first_levels(block, start, rows_each, got, out, low_at, up_at, time_at):
    for piece in range(rows_each // ROWS):
        rows = pl.ds(pl.multiple_of(start + piece * ROWS, ROWS), ROWS)
        value = got[block, pl.ds(piece * ROWS, ROWS)]
        for step in range(3):
            value = merge(value, value, step, rows, low_at, up_at, time_at)
        out[rows] = value


def pair_rows(pair, step, source, out, low_at, up_at, time_at):
    width = 2 << step
    start = pl.multiple_of(pair * 2 * ROWS, 2 * ROWS)
    trial = start % width
    base = start - trial
    low_row = pl.multiple_of(base + trial // 2, ROWS)
    up_row = pl.multiple_of(base + width // 2 + trial // 2, ROWS)
    for odd in range(2):
        rows = pl.ds(start + odd * ROWS, ROWS)
        move = 4 * odd if step >= 4 else 0
        lower = source[pl.ds(low_row + move, ROWS)]
        upper = source[pl.ds(up_row + move, ROWS)]
        out[rows] = merge(lower, upper, step, rows, low_at, up_at, time_at)


def scores(trials_ref, widths_ref, limit_ref, out_ref, bands, samples, chunk):
    boxes = out_ref.shape[1]
    source = lax.broadcasted_iota(jnp.int32, (samples, 2 * samples), 1) % samples
    target = lax.broadcasted_iota(jnp.int32, (samples, 2 * samples), 0)
    limit = limit_ref[0]
    kernels = []
    for box in range(boxes):
        width = widths_ref[box]
        back = target - source
        hit = jnp.where((back >= 0) & (back < width), 1.0, 0.0)
        mean = jnp.minimum(width, samples - source).astype(jnp.float32) * (1.0 / samples)
        kernels.append((hit - mean).astype(jnp.bfloat16))
    for part in range(bands // chunk):
        trials = trials_ref[pl.ds(part * chunk, chunk)]
        high = trials.astype(jnp.bfloat16)
        low = (trials - high.astype(jnp.float32)).astype(jnp.bfloat16)
        both = jnp.concatenate([high, low], axis=1)
        keep = lax.broadcasted_iota(jnp.int32, (1, chunk), 1) + part * chunk <= limit
        for box in range(boxes):
            offset = lax.dot_general(
                kernels[box], both, (((1,), (1,)), ((), ())), preferred_element_type=jnp.float32
            )
            top = jnp.max(offset, axis=0, keepdims=True)
            spread = jnp.sum(offset * offset, axis=0, keepdims=True) * (1.0 / samples)
            value = jnp.where(keep, top / jnp.sqrt(spread + 1e-05), 0.0)
            out_ref[0, pl.ds(box, 1), pl.ds(part * chunk, chunk)] = value


def kernel(
    beam_count, chan_count,
    x_ref, lower_ref, upper_ref, shift_ref, widths_ref, limit_ref, out_ref,
    sums, got, ping, pong, low_at, up_at, time_at, send_sem, recv_sem,
):
    count = beam_count * chan_count
    beam, chan = lax.axis_index("beam"), lax.axis_index("chan")
    me = beam * chan_count + chan
    channels, samples = x_ref.shape[1], x_ref.shape[2]
    rows_each = channels // SUB0
    bands = count * rows_each
    levels = bands.bit_length() - 1

    def partner(turn):
        chan_to = xor(chan, chan_count - 1 - turn // beam_count, chan_count)
        beam_to = xor(beam, beam_count - 1 - turn % beam_count, beam_count)
        return beam_to, chan_to

    barrier = pltpu.get_barrier_semaphore()

    def greet(turn, carry):
        pl.semaphore_signal(barrier, inc=1, device_id=partner(turn), device_id_type=MESH)
        return carry

    lax.fori_loop(0, count - 1, greet, 0)
    band = lax.broadcasted_iota(jnp.int32, (rows_each, channels), 0)
    channel = lax.broadcasted_iota(jnp.int32, (rows_each, channels), 1)
    adder = jnp.where(channel // SUB0 == band, 1.0, 0.0).astype(jnp.bfloat16)
    pl.semaphore_wait(barrier, count - 1)

    def copy_of(turn):
        return pltpu.make_async_remote_copy(
            src_ref=sums.at[turn],
            dst_ref=got.at[me],
            send_sem=send_sem.at[turn],
            recv_sem=recv_sem.at[turn],
            device_id=partner(turn),
            device_id_type=MESH,
        )

    def send(turn, carry):
        beam_to, chan_to = partner(turn)
        sums[turn] = jnp.dot(
            adder, x_ref[beam_to * chan_count + chan_to], preferred_element_type=jnp.float32
        )
        copy_of(turn).start()
        return carry

    lax.fori_loop(0, count - 1, send, 0)
    got[me] = jnp.dot(adder, x_ref[me], preferred_element_type=jnp.float32)
    build_indices(levels, bands, samples, lower_ref, upper_ref, shift_ref, low_at, up_at, time_at)
    ping[pl.ds(bands, ROWS)] = jnp.zeros((ROWS, samples), jnp.float32)
    pong[pl.ds(bands, ROWS)] = jnp.zeros((ROWS, samples), jnp.float32)

    def finish(turn, carry):
        copy_of(turn).wait()
        return carry

    lax.fori_loop(0, count - 1, finish, 0)

    def first(block, carry):
        first_levels(
            block, block * rows_each, rows_each, got, ping, low_at, up_at, time_at
        )
        return carry

    lax.fori_loop(0, count, first, 0)
    source, out = ping, pong
    for step in range(3, levels):
        def pairs(group, carry):
            for inner in range(4):
                pair_rows(4 * group + inner, step, source, out, low_at, up_at, time_at)
            return carry
        lax.fori_loop(0, bands // (8 * ROWS), pairs, 0)
        source, out = out, source
    scores(source, widths_ref, limit_ref, out_ref, bands, samples, 256)


def shards(intensities, lower_index, upper_index, delay_shift, widths, max_delay):
    beam_count = lax.axis_size("beam")
    chan_count = lax.axis_size("chan")
    count = beam_count * chan_count
    beams, channels, samples = intensities.shape
    rows_each = channels // SUB0
    bands = count * rows_each
    levels = lower_index.shape[0]
    vmem = pl.BlockSpec(memory_space=pltpu.VMEM)
    smem = pl.BlockSpec(memory_space=pltpu.SMEM)
    return pl.pallas_call(
        functools.partial(kernel, beam_count, chan_count),
        out_shape=jax.ShapeDtypeStruct((1, widths.shape[0], bands), jnp.float32),
        in_specs=[vmem] * 4 + [smem] * 2,
        out_specs=vmem,
        scratch_shapes=[
            pltpu.VMEM((count, rows_each, samples), jnp.float32),
            pltpu.VMEM((count, rows_each, samples), jnp.float32),
            pltpu.VMEM((bands + ROWS, samples), jnp.float32),
            pltpu.VMEM((bands + ROWS, samples), jnp.float32),
            pltpu.VMEM((levels, bands, samples), jnp.int32),
            pltpu.VMEM((levels, bands, samples), jnp.int32),
            pltpu.VMEM((levels, bands, samples), jnp.int32),
            pltpu.SemaphoreType.DMA((count,)),
            pltpu.SemaphoreType.DMA((count,)),
        ],
        compiler_params=pltpu.CompilerParams(
            collective_id=0, has_side_effects=True, vmem_limit_bytes=48 * 1024 * 1024
        ),
        name="search",
    )(intensities, lower_index, upper_index, delay_shift, widths, max_delay)


def solution(mesh):
    in_specs = (P(None, ("beam", "chan"), None), P(), P(), P(), P(), P(("beam", "chan")))
    out_specs = P(("beam", "chan"), None, None)
    return jax.shard_map(shards, mesh=mesh, in_specs=in_specs, out_specs=out_specs, check_vma=False)
```

```python
import functools

import jax
import jax.numpy as jnp
from jax import lax
from jax.experimental import pallas as pl
from jax.experimental.pallas import tpu as pltpu
from jax.sharding import PartitionSpec as P

SUB0 = 8
ROWS = 8
BATCH = 16
CHUNKS = 4
MESH = pl.DeviceIdType.MESH


def take(values, index, axis):
    return jnp.take_along_axis(values, index, axis=axis, mode="promise_in_bounds")


def build_indices(levels, bands, samples, lower_ref, upper_ref, shift_ref, low_at, up_at, time_at):
    depth = 16
    zeros = jnp.zeros((depth - levels, bands), jnp.int32)
    lower = jnp.concatenate([lower_ref[...], zeros], axis=0)
    upper = jnp.concatenate([upper_ref[...], zeros], axis=0)
    shift = jnp.concatenate([shift_ref[...], zeros], axis=0)
    level = lax.broadcasted_iota(jnp.int32, (depth, bands), 0)
    row = lax.broadcasted_iota(jnp.int32, (depth, bands), 1)
    width = jnp.left_shift(jnp.int32(2), level)
    trial = row & (width - 1)
    inside = (row & (ROWS - 1)) - trial
    skip = jnp.where(level >= 4, 4 * (trial // ROWS), 0)
    lower = jnp.where(level <= 2, inside + lower, lower - skip) & (ROWS - 1)
    upper = jnp.where(level <= 2, inside + width // 2 + upper, upper - skip) & (ROWS - 1)
    packed = jnp.concatenate(
        [(lower + ROWS * upper).astype(jnp.float32), jnp.minimum(shift, samples).astype(jnp.float32)],
        axis=0,
    ).astype(jnp.bfloat16)
    entry = lax.broadcasted_iota(jnp.int32, (2 * depth, samples), 0)
    time = lax.broadcasted_iota(jnp.int32, (bands, samples), 1)
    for step in range(levels):
        spread = jnp.where(entry == step, 256.0, jnp.where(entry == depth + step, 1.0, 0.0))
        value = lax.dot_general(
            packed,
            spread.astype(jnp.bfloat16),
            (((0,), (0,)), ((), ())),
            preferred_element_type=jnp.float32,
        ).astype(jnp.int32)
        low_at[step] = (value >> 8) & (ROWS - 1)
        up_at[step] = value >> 11
        time_at[step] = time - (value & 255)


def merge_rows(step, places, source, out, low_at, up_at, time_at):
    samples = out.shape[-1]
    for at in range(0, len(places), BATCH):
        batch = places[at : at + BATCH]
        outs = [pl.ds(row, ROWS) for row, _, _ in batch]
        lowers = [source[pl.ds(row, ROWS)] for _, row, _ in batch]
        uppers = [source[pl.ds(row, ROWS)] for _, _, row in batch]
        whens = [time_at[step, rows] for rows in outs]
        uppers = [take(v, up_at[step, rows], 0) for v, rows in zip(uppers, outs)]
        lowers = [take(v, low_at[step, rows], 0) for v, rows in zip(lowers, outs)]
        uppers = [take(v, when & (samples - 1), 1) for v, when in zip(uppers, whens)]
        for rows, lower, upper, when in zip(outs, lowers, uppers, whens):
            out[rows] = lower + jnp.where(when >= 0, upper, 0.0)


def places_of(step, start, size):
    width = 2 << step
    places = []
    for offset in range(0, size, ROWS):
        row = start + offset
        if width <= ROWS:
            places.append((row, row, row))
            continue
        trial = offset % width
        skip = 4 * (trial // ROWS) if step >= 4 else 0
        base = offset - trial
        places.append((row, start + base + skip, start + base + width // 2 + skip))
    return places


def scores(trials_ref, widths_ref, limit_ref, out_ref, bands, samples, chunk):
    boxes = out_ref.shape[1]
    source = lax.broadcasted_iota(jnp.int32, (samples, 2 * samples), 1) % samples
    target = lax.broadcasted_iota(jnp.int32, (samples, 2 * samples), 0)
    limit = limit_ref[0]
    kernels = []
    for box in range(boxes):
        width = widths_ref[box]
        back = target - source
        hit = jnp.where((back >= 0) & (back < width), 1.0, 0.0)
        mean = jnp.minimum(width, samples - source).astype(jnp.float32) * (1.0 / samples)
        kernels.append((hit - mean).astype(jnp.bfloat16))
    for part in range(bands // chunk):
        trials = trials_ref[pl.ds(part * chunk, chunk)]
        high = trials.astype(jnp.bfloat16)
        low = (trials - high.astype(jnp.float32)).astype(jnp.bfloat16)
        both = jnp.concatenate([high, low], axis=1)
        keep = lax.broadcasted_iota(jnp.int32, (1, chunk), 1) + part * chunk <= limit
        for box in range(boxes):
            offset = lax.dot_general(
                kernels[box], both, (((1,), (1,)), ((), ())), preferred_element_type=jnp.float32
            )
            top = jnp.max(offset, axis=0, keepdims=True)
            spread = jnp.sum(offset * offset, axis=0, keepdims=True) * (1.0 / samples)
            value = jnp.where(keep, top / jnp.sqrt(spread + 1e-05), 0.0)
            out_ref[0, pl.ds(box, 1), pl.ds(part * chunk, chunk)] = value


def kernel(
    beam_count, chan_count, levels,
    x_hbm, lower_hbm, upper_hbm, shift_hbm, widths_hbm, limit_hbm, out_ref,
    x_ref, lower_ref, upper_ref, shift_ref, widths_ref, limit_ref, sums, got, *rest,
):
    states, (low_at, up_at, time_at, load_sem, send_sem, recv_sem) = rest[:levels], rest[levels:]
    count = beam_count * chan_count
    beam, chan = lax.axis_index("beam"), lax.axis_index("chan")
    me = beam * chan_count + chan
    channels, samples = x_ref.shape[1], x_ref.shape[2]
    rows_each = channels // SUB0
    bands = count * rows_each
    beams_each = count // CHUNKS

    def flips(value, size):
        return [(1 << bit) * (1 - 2 * (value // (1 << bit) % 2)) for bit in range(size.bit_length() - 1)]

    beam_flips, chan_flips = flips(beam, beam_count), flips(chan, chan_count)

    def xor(value, steps, mask):
        for bit, step in enumerate(steps):
            if mask >> bit & 1:
                value = value + step
        return value

    turns = [(c, b) for c in reversed(range(chan_count)) for b in range(beam_count) if (c, b) != (0, 0)]

    def partner(c, b):
        return xor(beam, beam_flips, b), xor(chan, chan_flips, c)

    barrier = pltpu.get_barrier_semaphore()
    loads = [
        pltpu.make_async_copy(
            x_hbm.at[pl.ds(part * beams_each, beams_each)],
            x_ref.at[pl.ds(part * beams_each, beams_each)],
            load_sem.at[part],
        )
        for part in range(CHUNKS)
    ]
    others = [(lower_hbm, lower_ref), (upper_hbm, upper_ref), (shift_hbm, shift_ref), (widths_hbm, widths_ref), (limit_hbm, limit_ref)]
    tables = [
        pltpu.make_async_copy(source, target, load_sem.at[CHUNKS + at])
        for at, (source, target) in enumerate(others)
    ]
    for load in loads + tables:
        load.start()
    for c, b in turns:
        pl.semaphore_signal(barrier, inc=1, device_id=partner(c, b), device_id_type=MESH)

    band = lax.broadcasted_iota(jnp.int32, (rows_each, channels), 0)
    channel = lax.broadcasted_iota(jnp.int32, (rows_each, channels), 1)
    adder = jnp.where(channel // SUB0 == band, 1.0, 0.0).astype(jnp.bfloat16)
    for part, load in enumerate(loads):
        load.wait()
        for owner in range(part * beams_each, (part + 1) * beams_each):
            sums[owner] = jnp.dot(adder, x_ref[owner], preferred_element_type=jnp.float32)
    for load in tables:
        load.wait()
    pl.semaphore_wait(barrier, count - 1)

    copies = {}
    for c, b in turns:
        beam_to, chan_to = partner(c, b)
        copies[c, b] = pltpu.make_async_remote_copy(
            src_ref=sums.at[beam_to * chan_count + chan_to],
            dst_ref=got.at[me],
            send_sem=send_sem.at[c * beam_count + b],
            recv_sem=recv_sem.at[c * beam_count + b],
            device_id=(beam_to, chan_to),
            device_id_type=MESH,
        )
        copies[c, b].start()
    got[me] = sums[me]
    build_indices(levels, bands, samples, lower_ref, upper_ref, shift_ref, low_at, up_at, time_at)
    for state in states:
        state[pl.ds(bands, ROWS)] = jnp.zeros((ROWS, samples), jnp.float32)

    def level(step, starts, size):
        places = []
        for start in starts:
            places += places_of(step, start, size)
        merge_rows(step, places, states[step - 1], states[step], low_at, up_at, time_at)

    local = rows_each.bit_length() - 1
    group = chan_count * rows_each
    for c in range(chan_count):
        for b in range(beam_count):
            if (c, b) != (0, 0):
                copies[c, b].wait_recv()
        chan_from = xor(chan, chan_flips, c)
        where = pl.multiple_of(chan_from * rows_each, rows_each)
        places = []
        values = []
        for b in range(beam_count):
            for piece in range(0, rows_each, ROWS):
                places.append(b * group + where + piece)
                values.append(got[b * chan_count + chan_from, pl.ds(piece, ROWS)])
        for step in range(min(3, local)):
            rows = [pl.ds(place, ROWS) for place in places]
            whens = [time_at[step, at] for at in rows]
            uppers = [take(v, up_at[step, at], 0) for v, at in zip(values, rows)]
            uppers = [take(v, when & (samples - 1), 1) for v, when in zip(uppers, whens)]
            lowers = [take(v, low_at[step, at], 0) for v, at in zip(values, rows)]
            values = [v + jnp.where(when >= 0, u, 0.0) for v, u, when in zip(lowers, uppers, whens)]
        for place, value in zip(places, values):
            states[2][pl.ds(place, ROWS)] = value
        for step in range(3, local):
            level(step, [b * group + where for b in range(beam_count)], rows_each)
        depth = 0
        while (c + 1) % (2 << depth) == 0 and (2 << depth) <= chan_count:
            size = rows_each * (2 << depth)
            first = chan_from // (2 << depth) * size
            first = pl.multiple_of(first, size)
            level(local + depth, [b * group + first for b in range(beam_count)], size)
            depth += 1
    for step in range(local + chan_count.bit_length() - 1, levels):
        level(step, [0], bands)
    for c, b in turns:
        copies[c, b].wait_send()
    scores(states[levels - 1], widths_ref, limit_ref, out_ref, bands, samples, 256)


def shards(intensities, lower_index, upper_index, delay_shift, widths, max_delay):
    beam_count = lax.axis_size("beam")
    chan_count = lax.axis_size("chan")
    count = beam_count * chan_count
    beams, channels, samples = intensities.shape
    rows_each = channels // SUB0
    bands = count * rows_each
    levels = lower_index.shape[0]
    anywhere = pl.BlockSpec(memory_space=pl.ANY)
    return pl.pallas_call(
        functools.partial(kernel, beam_count, chan_count, levels),
        out_shape=jax.ShapeDtypeStruct((1, widths.shape[0], bands), jnp.float32),
        in_specs=[anywhere] * 6,
        out_specs=pl.BlockSpec(memory_space=pltpu.VMEM),
        scratch_shapes=[
            pltpu.VMEM((beams, channels, samples), intensities.dtype),
            pltpu.VMEM(lower_index.shape, jnp.int32),
            pltpu.VMEM(upper_index.shape, jnp.int32),
            pltpu.VMEM(delay_shift.shape, jnp.int32),
            pltpu.SMEM(widths.shape, jnp.int32),
            pltpu.SMEM(max_delay.shape, jnp.int32),
            pltpu.VMEM((count, rows_each, samples), jnp.float32),
            pltpu.VMEM((count, rows_each, samples), jnp.float32),
        ]
        + [pltpu.VMEM((bands + ROWS, samples), jnp.float32)] * levels
        + [pltpu.VMEM((levels, bands, samples), jnp.int32)] * 3
        + [
            pltpu.SemaphoreType.DMA((CHUNKS + 5,)),
            pltpu.SemaphoreType.DMA((count,)),
            pltpu.SemaphoreType.DMA((count,)),
        ],
        compiler_params=pltpu.CompilerParams(
            collective_id=0, has_side_effects=True, vmem_limit_bytes=56 * 1024 * 1024
        ),
        name="search",
    )(intensities, lower_index, upper_index, delay_shift, widths, max_delay)


def solution(mesh):
    in_specs = (P(None, ("beam", "chan"), None), P(), P(), P(), P(), P(("beam", "chan")))
    out_specs = P(("beam", "chan"), None, None)
    return jax.shard_map(shards, mesh=mesh, in_specs=in_specs, out_specs=out_specs, check_vma=False)
```

```python
import functools

import jax
import jax.numpy as jnp
from jax import lax
from jax.experimental import pallas as pl
from jax.experimental.pallas import tpu as pltpu
from jax.sharding import PartitionSpec as P

SUB0 = 8
ROWS = 8
BATCH = 16
CHUNKS = 4
MESH = pl.DeviceIdType.MESH


def take(values, index, axis):
    return jnp.take_along_axis(values, index, axis=axis, mode="promise_in_bounds")


def build_indices(levels, bands, samples, lower_ref, upper_ref, shift_ref, low_at, up_at, time_at):
    depth = 16
    zeros = jnp.zeros((depth - levels, bands), jnp.int32)
    lower = jnp.concatenate([lower_ref[...], zeros], axis=0)
    upper = jnp.concatenate([upper_ref[...], zeros], axis=0)
    shift = jnp.concatenate([shift_ref[...], zeros], axis=0)
    level = lax.broadcasted_iota(jnp.int32, (depth, bands), 0)
    row = lax.broadcasted_iota(jnp.int32, (depth, bands), 1)
    width = jnp.left_shift(jnp.int32(2), level)
    trial = row & (width - 1)
    inside = (row & (ROWS - 1)) - trial
    skip = jnp.where(level >= 4, 4 * (trial // ROWS), 0)
    lower = jnp.where(level <= 2, inside + lower, lower - skip) & (ROWS - 1)
    upper = jnp.where(level <= 2, inside + width // 2 + upper, upper - skip) & (ROWS - 1)
    packed = jnp.concatenate(
        [(lower + ROWS * upper).astype(jnp.float32), jnp.minimum(shift, samples).astype(jnp.float32)],
        axis=0,
    ).astype(jnp.bfloat16)
    entry = lax.broadcasted_iota(jnp.int32, (2 * depth, samples), 0)
    time = lax.broadcasted_iota(jnp.int32, (bands, samples), 1)
    for step in range(levels):
        spread = jnp.where(entry == step, 256.0, jnp.where(entry == depth + step, 1.0, 0.0))
        value = lax.dot_general(
            packed,
            spread.astype(jnp.bfloat16),
            (((0,), (0,)), ((), ())),
            preferred_element_type=jnp.float32,
        ).astype(jnp.int32)
        low_at[step] = (value >> 8) & (ROWS - 1)
        up_at[step] = value >> 11
        time_at[step] = time - (value & 255)


def merge_rows(step, places, source, out, low_at, up_at, time_at):
    samples = out.shape[-1]
    for at in range(0, len(places), BATCH):
        batch = places[at : at + BATCH]
        outs = [pl.ds(row, ROWS) for row, _, _ in batch]
        lowers = [source[pl.ds(row, ROWS)] for _, row, _ in batch]
        uppers = [source[pl.ds(row, ROWS)] for _, _, row in batch]
        whens = [time_at[step, rows] for rows in outs]
        uppers = [take(v, up_at[step, rows], 0) for v, rows in zip(uppers, outs)]
        lowers = [take(v, low_at[step, rows], 0) for v, rows in zip(lowers, outs)]
        uppers = [take(v, when & (samples - 1), 1) for v, when in zip(uppers, whens)]
        for rows, lower, upper, when in zip(outs, lowers, uppers, whens):
            out[rows] = lower + jnp.where(when >= 0, upper, 0.0)


def places_of(step, start, size):
    width = 2 << step
    places = []
    for offset in range(0, size, ROWS):
        row = start + offset
        if width <= ROWS:
            places.append((row, row, row))
            continue
        trial = offset % width
        skip = 4 * (trial // ROWS) if step >= 4 else 0
        base = offset - trial
        places.append((row, start + base + skip, start + base + width // 2 + skip))
    return places


def scores(trials_ref, widths_ref, limit_ref, out_ref, bands, samples, chunk):
    boxes = out_ref.shape[1]
    source = lax.broadcasted_iota(jnp.int32, (samples, 2 * samples), 1) % samples
    target = lax.broadcasted_iota(jnp.int32, (samples, 2 * samples), 0)
    limit = limit_ref[0]
    kernels = []
    for box in range(boxes):
        width = widths_ref[box]
        back = target - source
        hit = jnp.where((back >= 0) & (back < width), 1.0, 0.0)
        mean = jnp.minimum(width, samples - source).astype(jnp.float32) * (1.0 / samples)
        kernels.append((hit - mean).astype(jnp.bfloat16))
    for part in range(bands // chunk):
        trials = trials_ref[pl.ds(part * chunk, chunk)]
        high = trials.astype(jnp.bfloat16)
        low = (trials - high.astype(jnp.float32)).astype(jnp.bfloat16)
        both = jnp.concatenate([high, low], axis=1)
        keep = lax.broadcasted_iota(jnp.int32, (1, chunk), 1) + part * chunk <= limit
        for box in range(boxes):
            offset = lax.dot_general(
                kernels[box], both, (((1,), (1,)), ((), ())), preferred_element_type=jnp.float32
            )
            top = jnp.max(offset, axis=0, keepdims=True)
            spread = jnp.sum(offset * offset, axis=0, keepdims=True) * (1.0 / samples)
            value = jnp.where(keep, top / jnp.sqrt(spread + 1e-05), 0.0)
            out_ref[0, pl.ds(box, 1), pl.ds(part * chunk, chunk)] = value


def kernel(
    beam_count, chan_count, levels,
    x_hbm, lower_hbm, upper_hbm, shift_hbm, widths_hbm, limit_hbm, out_ref,
    x_ref, lower_ref, upper_ref, shift_ref, widths_ref, limit_ref, sums, got, *rest,
):
    states, (low_at, up_at, time_at, load_sem, send_sem, recv_sem) = rest[:levels], rest[levels:]
    count = beam_count * chan_count
    beam, chan = lax.axis_index("beam"), lax.axis_index("chan")
    me = beam * chan_count + chan
    channels, samples = x_ref.shape[1], x_ref.shape[2]
    rows_each = channels // SUB0
    bands = count * rows_each
    beams_each = count // CHUNKS

    def flips(value, size):
        return [(1 << bit) * (1 - 2 * (value // (1 << bit) % 2)) for bit in range(size.bit_length() - 1)]

    beam_flips, chan_flips = flips(beam, beam_count), flips(chan, chan_count)

    def xor(value, steps, mask):
        for bit, step in enumerate(steps):
            if mask >> bit & 1:
                value = value + step
        return value

    turns = [(c, b) for c in range(chan_count) for b in range(beam_count) if (c, b) != (0, 0)]

    def partner(c, b):
        return xor(beam, beam_flips, b), xor(chan, chan_flips, c)

    barrier = pltpu.get_barrier_semaphore()
    loads = [
        pltpu.make_async_copy(
            x_hbm.at[pl.ds(part * beams_each, beams_each)],
            x_ref.at[pl.ds(part * beams_each, beams_each)],
            load_sem.at[part],
        )
        for part in range(CHUNKS)
    ]
    others = [(lower_hbm, lower_ref), (upper_hbm, upper_ref), (shift_hbm, shift_ref), (widths_hbm, widths_ref), (limit_hbm, limit_ref)]
    tables = [
        pltpu.make_async_copy(source, target, load_sem.at[CHUNKS + at])
        for at, (source, target) in enumerate(others)
    ]
    for load in loads + tables:
        load.start()
    for c, b in turns:
        pl.semaphore_signal(barrier, inc=1, device_id=partner(c, b), device_id_type=MESH)

    band = lax.broadcasted_iota(jnp.int32, (rows_each, channels), 0)
    channel = lax.broadcasted_iota(jnp.int32, (rows_each, channels), 1)
    adder = jnp.where(channel // SUB0 == band, 1.0, 0.0).astype(jnp.bfloat16)
    for part, load in enumerate(loads):
        load.wait()
        for owner in range(part * beams_each, (part + 1) * beams_each):
            sums[owner] = jnp.dot(adder, x_ref[owner], preferred_element_type=jnp.float32)
    for load in tables:
        load.wait()
    pl.semaphore_wait(barrier, count - 1)

    copies = {}
    for c, b in turns:
        beam_to, chan_to = partner(c, b)
        copies[c, b] = pltpu.make_async_remote_copy(
            src_ref=sums.at[beam_to * chan_count + chan_to],
            dst_ref=got.at[me],
            send_sem=send_sem.at[c * beam_count + b],
            recv_sem=recv_sem.at[c * beam_count + b],
            device_id=(beam_to, chan_to),
            device_id_type=MESH,
        )
        copies[c, b].start()
    got[me] = sums[me]
    build_indices(levels, bands, samples, lower_ref, upper_ref, shift_ref, low_at, up_at, time_at)
    for state in states:
        state[pl.ds(bands, ROWS)] = jnp.zeros((ROWS, samples), jnp.float32)

    def level(step, starts, size):
        places = []
        for start in starts:
            places += places_of(step, start, size)
        merge_rows(step, places, states[step - 1], states[step], low_at, up_at, time_at)

    local = rows_each.bit_length() - 1
    group = chan_count * rows_each
    for c in range(chan_count):
        for b in range(beam_count):
            if (c, b) != (0, 0):
                copies[c, b].wait_recv()
        chan_from = xor(chan, chan_flips, c)
        where = pl.multiple_of(chan_from * rows_each, rows_each)
        places = []
        values = []
        for b in range(beam_count):
            for piece in range(0, rows_each, ROWS):
                places.append(b * group + where + piece)
                values.append(got[b * chan_count + chan_from, pl.ds(piece, ROWS)])
        for step in range(min(3, local)):
            rows = [pl.ds(place, ROWS) for place in places]
            whens = [time_at[step, at] for at in rows]
            uppers = [take(v, up_at[step, at], 0) for v, at in zip(values, rows)]
            uppers = [take(v, when & (samples - 1), 1) for v, when in zip(uppers, whens)]
            lowers = [take(v, low_at[step, at], 0) for v, at in zip(values, rows)]
            values = [v + jnp.where(when >= 0, u, 0.0) for v, u, when in zip(lowers, uppers, whens)]
        for place, value in zip(places, values):
            states[2][pl.ds(place, ROWS)] = value
        for step in range(3, local):
            level(step, [b * group + where for b in range(beam_count)], rows_each)
        depth = 0
        while (c + 1) % (2 << depth) == 0 and (2 << depth) <= chan_count:
            size = rows_each * (2 << depth)
            first = chan_from // (2 << depth) * size
            first = pl.multiple_of(first, size)
            level(local + depth, [b * group + first for b in range(beam_count)], size)
            depth += 1
    for step in range(local + chan_count.bit_length() - 1, levels):
        level(step, [0], bands)
    for c, b in turns:
        copies[c, b].wait_send()
    scores(states[levels - 1], widths_ref, limit_ref, out_ref, bands, samples, 256)


def shards(intensities, lower_index, upper_index, delay_shift, widths, max_delay):
    beam_count = lax.axis_size("beam")
    chan_count = lax.axis_size("chan")
    count = beam_count * chan_count
    beams, channels, samples = intensities.shape
    rows_each = channels // SUB0
    bands = count * rows_each
    levels = lower_index.shape[0]
    anywhere = pl.BlockSpec(memory_space=pl.ANY)
    return pl.pallas_call(
        functools.partial(kernel, beam_count, chan_count, levels),
        out_shape=jax.ShapeDtypeStruct((1, widths.shape[0], bands), jnp.float32),
        in_specs=[anywhere] * 6,
        out_specs=pl.BlockSpec(memory_space=pltpu.VMEM),
        scratch_shapes=[
            pltpu.VMEM((beams, channels, samples), intensities.dtype),
            pltpu.VMEM(lower_index.shape, jnp.int32),
            pltpu.VMEM(upper_index.shape, jnp.int32),
            pltpu.VMEM(delay_shift.shape, jnp.int32),
            pltpu.SMEM(widths.shape, jnp.int32),
            pltpu.SMEM(max_delay.shape, jnp.int32),
            pltpu.VMEM((count, rows_each, samples), jnp.float32),
            pltpu.VMEM((count, rows_each, samples), jnp.float32),
        ]
        + [pltpu.VMEM((bands + ROWS, samples), jnp.float32)] * levels
        + [pltpu.VMEM((levels, bands, samples), jnp.int32)] * 3
        + [
            pltpu.SemaphoreType.DMA((CHUNKS + 5,)),
            pltpu.SemaphoreType.DMA((count,)),
            pltpu.SemaphoreType.DMA((count,)),
        ],
        compiler_params=pltpu.CompilerParams(
            collective_id=0, has_side_effects=True, vmem_limit_bytes=56 * 1024 * 1024
        ),
        name="search",
    )(intensities, lower_index, upper_index, delay_shift, widths, max_delay)


def solution(mesh):
    in_specs = (P(None, ("beam", "chan"), None), P(), P(), P(), P(), P(("beam", "chan")))
    out_specs = P(("beam", "chan"), None, None)
    return jax.shard_map(shards, mesh=mesh, in_specs=in_specs, out_specs=out_specs, check_vma=False)
```

```python
import functools

import jax
import jax.numpy as jnp
from jax import lax
from jax.experimental import pallas as pl
from jax.experimental.pallas import tpu as pltpu
from jax.sharding import PartitionSpec as P

SUB0 = 8
ROWS = 8
BATCH = 16
CHUNKS = 4
MESH = pl.DeviceIdType.MESH


def take(values, index, axis):
    return jnp.take_along_axis(values, index, axis=axis, mode="promise_in_bounds")


def build_indices(levels, bands, samples, lower_ref, upper_ref, shift_ref, low_at, up_at, time_at):
    depth = 16
    zeros = jnp.zeros((depth - levels, bands), jnp.int32)
    lower = jnp.concatenate([lower_ref[...], zeros], axis=0)
    upper = jnp.concatenate([upper_ref[...], zeros], axis=0)
    shift = jnp.concatenate([shift_ref[...], zeros], axis=0)
    level = lax.broadcasted_iota(jnp.int32, (depth, bands), 0)
    row = lax.broadcasted_iota(jnp.int32, (depth, bands), 1)
    width = jnp.left_shift(jnp.int32(2), level)
    trial = row & (width - 1)
    inside = (row & (ROWS - 1)) - trial
    skip = jnp.where(level >= 4, 4 * (trial // ROWS), 0)
    lower = jnp.where(level <= 2, inside + lower, lower - skip) & (ROWS - 1)
    upper = jnp.where(level <= 2, inside + width // 2 + upper, upper - skip) & (ROWS - 1)
    packed = jnp.concatenate(
        [(lower + ROWS * upper).astype(jnp.float32), jnp.minimum(shift, samples).astype(jnp.float32)],
        axis=0,
    ).astype(jnp.bfloat16)
    entry = lax.broadcasted_iota(jnp.int32, (2 * depth, samples), 0)
    time = lax.broadcasted_iota(jnp.int32, (bands, samples), 1)
    for step in range(levels):
        spread = jnp.where(entry == step, 256.0, jnp.where(entry == depth + step, 1.0, 0.0))
        value = lax.dot_general(
            packed,
            spread.astype(jnp.bfloat16),
            (((0,), (0,)), ((), ())),
            preferred_element_type=jnp.float32,
        ).astype(jnp.int32)
        low_at[step] = (value >> 8) & (ROWS - 1)
        up_at[step] = value >> 11
        time_at[step] = time - (value & 255)


def merge_rows(step, places, source, out, low_at, up_at, time_at):
    samples = out.shape[-1]
    for at in range(0, len(places), BATCH):
        batch = places[at : at + BATCH]
        outs = [pl.ds(row, ROWS) for row, _, _ in batch]
        lowers = [source[pl.ds(row, ROWS)] for _, row, _ in batch]
        uppers = [source[pl.ds(row, ROWS)] for _, _, row in batch]
        whens = [time_at[step, rows] for rows in outs]
        uppers = [take(v, up_at[step, rows], 0) for v, rows in zip(uppers, outs)]
        lowers = [take(v, low_at[step, rows], 0) for v, rows in zip(lowers, outs)]
        uppers = [take(v, when & (samples - 1), 1) for v, when in zip(uppers, whens)]
        for rows, lower, upper, when in zip(outs, lowers, uppers, whens):
            out[rows] = lower + jnp.where(when >= 0, upper, 0.0)


def places_of(step, start, size):
    width = 2 << step
    places = []
    for offset in range(0, size, ROWS):
        row = start + offset
        if width <= ROWS:
            places.append((row, row, row))
            continue
        trial = offset % width
        skip = 4 * (trial // ROWS) if step >= 4 else 0
        base = offset - trial
        places.append((row, start + base + skip, start + base + width // 2 + skip))
    return places


def scores(trials_ref, widths_ref, limit_ref, out_ref, bands, samples, chunk):
    boxes = out_ref.shape[1]
    source = lax.broadcasted_iota(jnp.int32, (samples, 2 * samples), 1) % samples
    target = lax.broadcasted_iota(jnp.int32, (samples, 2 * samples), 0)
    limit = limit_ref[0]
    kernels = []
    for box in range(boxes):
        width = widths_ref[box]
        back = target - source
        hit = jnp.where((back >= 0) & (back < width), 1.0, 0.0)
        mean = jnp.minimum(width, samples - source).astype(jnp.float32) * (1.0 / samples)
        kernels.append((hit - mean).astype(jnp.bfloat16))
    for part in range(bands // chunk):
        trials = trials_ref[pl.ds(part * chunk, chunk)]
        high = trials.astype(jnp.bfloat16)
        low = (trials - high.astype(jnp.float32)).astype(jnp.bfloat16)
        both = jnp.concatenate([high, low], axis=1)
        keep = lax.broadcasted_iota(jnp.int32, (1, chunk), 1) + part * chunk <= limit
        for box in range(boxes):
            offset = lax.dot_general(
                kernels[box], both, (((1,), (1,)), ((), ())), preferred_element_type=jnp.float32
            )
            top = jnp.max(offset, axis=0, keepdims=True)
            spread = jnp.sum(offset * offset, axis=0, keepdims=True) * (1.0 / samples)
            value = jnp.where(keep, top / jnp.sqrt(spread + 1e-05), 0.0)
            out_ref[0, pl.ds(box, 1), pl.ds(part * chunk, chunk)] = value


def kernel(
    beam_count, chan_count, levels,
    x_hbm, lower_hbm, upper_hbm, shift_hbm, widths_hbm, limit_hbm, out_ref,
    x_ref, lower_ref, upper_ref, shift_ref, widths_ref, limit_ref, sums, got, *rest,
):
    states, (low_at, up_at, time_at, load_sem, send_sem, recv_sem) = rest[:levels], rest[levels:]
    count = beam_count * chan_count
    beam, chan = lax.axis_index("beam"), lax.axis_index("chan")
    me = beam * chan_count + chan
    channels, samples = x_ref.shape[1], x_ref.shape[2]
    rows_each = channels // SUB0
    bands = count * rows_each
    beams_each = count // CHUNKS

    def flips(value, size):
        return [(1 << bit) * (1 - 2 * (value // (1 << bit) % 2)) for bit in range(size.bit_length() - 1)]

    beam_flips, chan_flips = flips(beam, beam_count), flips(chan, chan_count)

    def xor(value, steps, mask):
        for bit, step in enumerate(steps):
            if mask >> bit & 1:
                value = value + step
        return value

    turns = [(c, b) for c in range(chan_count) for b in range(beam_count) if (c, b) != (0, 0)]

    def partner(c, b):
        return xor(beam, beam_flips, b), xor(chan, chan_flips, c)

    barrier = pltpu.get_barrier_semaphore()
    loads = [
        pltpu.make_async_copy(
            x_hbm.at[pl.ds(part * beams_each, beams_each)],
            x_ref.at[pl.ds(part * beams_each, beams_each)],
            load_sem.at[part],
        )
        for part in range(CHUNKS)
    ]
    others = [(lower_hbm, lower_ref), (upper_hbm, upper_ref), (shift_hbm, shift_ref), (widths_hbm, widths_ref), (limit_hbm, limit_ref)]
    tables = [
        pltpu.make_async_copy(source, target, load_sem.at[CHUNKS + at])
        for at, (source, target) in enumerate(others)
    ]
    for load in loads + tables:
        load.start()
    for c, b in reversed(turns):
        pl.semaphore_signal(barrier, inc=1, device_id=partner(c, b), device_id_type=MESH)

    band = lax.broadcasted_iota(jnp.int32, (rows_each, channels), 0)
    channel = lax.broadcasted_iota(jnp.int32, (rows_each, channels), 1)
    adder = jnp.where(channel // SUB0 == band, 1.0, 0.0).astype(jnp.bfloat16)
    for part, load in enumerate(loads):
        load.wait()
        for owner in range(part * beams_each, (part + 1) * beams_each):
            sums[owner] = jnp.dot(adder, x_ref[owner], preferred_element_type=jnp.float32)
    for load in tables:
        load.wait()
    pl.semaphore_wait(barrier, count - 1)

    copies = {}
    for c, b in turns:
        beam_to, chan_to = partner(c, b)
        copies[c, b] = pltpu.make_async_remote_copy(
            src_ref=sums.at[beam_to * chan_count + chan_to],
            dst_ref=got.at[me],
            send_sem=send_sem.at[c * beam_count + b],
            recv_sem=recv_sem.at[c * beam_count + b],
            device_id=(beam_to, chan_to),
            device_id_type=MESH,
        )
        copies[c, b].start()
    got[me] = sums[me]
    build_indices(levels, bands, samples, lower_ref, upper_ref, shift_ref, low_at, up_at, time_at)
    for state in states:
        state[pl.ds(bands, ROWS)] = jnp.zeros((ROWS, samples), jnp.float32)

    def level(step, starts, size):
        places = []
        for start in starts:
            places += places_of(step, start, size)
        merge_rows(step, places, states[step - 1], states[step], low_at, up_at, time_at)

    local = rows_each.bit_length() - 1
    group = chan_count * rows_each
    for c in range(chan_count):
        for b in range(beam_count):
            if (c, b) != (0, 0):
                copies[c, b].wait_recv()
        chan_from = xor(chan, chan_flips, c)
        where = pl.multiple_of(chan_from * rows_each, rows_each)
        places = []
        values = []
        for b in range(beam_count):
            for piece in range(0, rows_each, ROWS):
                places.append(b * group + where + piece)
                values.append(got[b * chan_count + chan_from, pl.ds(piece, ROWS)])
        for step in range(min(3, local)):
            rows = [pl.ds(place, ROWS) for place in places]
            whens = [time_at[step, at] for at in rows]
            uppers = [take(v, up_at[step, at], 0) for v, at in zip(values, rows)]
            uppers = [take(v, when & (samples - 1), 1) for v, when in zip(uppers, whens)]
            lowers = [take(v, low_at[step, at], 0) for v, at in zip(values, rows)]
            values = [v + jnp.where(when >= 0, u, 0.0) for v, u, when in zip(lowers, uppers, whens)]
        for place, value in zip(places, values):
            states[2][pl.ds(place, ROWS)] = value
        for step in range(3, local):
            level(step, [b * group + where for b in range(beam_count)], rows_each)
        depth = 0
        while (c + 1) % (2 << depth) == 0 and (2 << depth) <= chan_count:
            size = rows_each * (2 << depth)
            first = chan_from // (2 << depth) * size
            first = pl.multiple_of(first, size)
            level(local + depth, [b * group + first for b in range(beam_count)], size)
            depth += 1
    for step in range(local + chan_count.bit_length() - 1, levels):
        level(step, [0], bands)
    scores(states[levels - 1], widths_ref, limit_ref, out_ref, bands, samples, 256)
    for c, b in turns:
        copies[c, b].wait_send()


def shards(intensities, lower_index, upper_index, delay_shift, widths, max_delay):
    beam_count = lax.axis_size("beam")
    chan_count = lax.axis_size("chan")
    count = beam_count * chan_count
    beams, channels, samples = intensities.shape
    rows_each = channels // SUB0
    bands = count * rows_each
    levels = lower_index.shape[0]
    anywhere = pl.BlockSpec(memory_space=pl.ANY)
    return pl.pallas_call(
        functools.partial(kernel, beam_count, chan_count, levels),
        out_shape=jax.ShapeDtypeStruct((1, widths.shape[0], bands), jnp.float32),
        in_specs=[anywhere] * 6,
        out_specs=pl.BlockSpec(memory_space=pltpu.VMEM),
        scratch_shapes=[
            pltpu.VMEM((beams, channels, samples), intensities.dtype),
            pltpu.VMEM(lower_index.shape, jnp.int32),
            pltpu.VMEM(upper_index.shape, jnp.int32),
            pltpu.VMEM(delay_shift.shape, jnp.int32),
            pltpu.SMEM(widths.shape, jnp.int32),
            pltpu.SMEM(max_delay.shape, jnp.int32),
            pltpu.VMEM((count, rows_each, samples), jnp.float32),
            pltpu.VMEM((count, rows_each, samples), jnp.float32),
        ]
        + [pltpu.VMEM((bands + ROWS, samples), jnp.float32)] * levels
        + [pltpu.VMEM((levels, bands, samples), jnp.int32)] * 3
        + [
            pltpu.SemaphoreType.DMA((CHUNKS + 5,)),
            pltpu.SemaphoreType.DMA((count,)),
            pltpu.SemaphoreType.DMA((count,)),
        ],
        compiler_params=pltpu.CompilerParams(
            collective_id=0, has_side_effects=True, vmem_limit_bytes=56 * 1024 * 1024
        ),
        name="search",
    )(intensities, lower_index, upper_index, delay_shift, widths, max_delay)


def solution(mesh):
    in_specs = (P(None, ("beam", "chan"), None), P(), P(), P(), P(), P(("beam", "chan")))
    out_specs = P(("beam", "chan"), None, None)
    return jax.shard_map(shards, mesh=mesh, in_specs=in_specs, out_specs=out_specs, check_vma=False)
```
